32 devices in a mesh: groups: 2 (over x), shard: 16 (over z, y, core).
Axes of the slice: x: 2, y: 2, z: 4, core: 2. Of those that a mesh axis runs over, the one named last changes fastest.
Arguments:
- test_grads: bfloat16 [512, 8192], P(('groups', 'shard')), parts along dimension 0
- train_grads: bfloat16 [24576, 8192], P(('groups', 'shard')), parts along dimension 0
- candidates: int32 [512, 4], P(('groups', 'shard')), parts along dimension 0, may hold values from 0 to 15, all different within a row; in each aligned block of 16 rows (0 to 15, 16 to 31, ...) at most 4 rows name the same one
- owner: int32 [32], P('groups'), parts along dimension 0, may hold values from 0 to 15, each once
- cluster_sizes: int32 [32], P('groups'), parts along dimension 0, may hold values from 384 to 768, as said below
Outputs:
- influence: float32 [512, 4, 768], P(('groups', 'shard')), parts along dimension 0
The draws below stay inside these ranges and needn't reach their ends.
There are 2 independent parts, one for each index of `groups`. The reference program is written for one: setup_inputs(seed, part) draws one part's arguments, and reference() takes and returns one part's arrays. A program takes and returns all parts, laid end to end along the dimension named above; each array names one. Nothing has to cross between parts.
Inputs may be any that keep to these rules, and one draw needn't show every extreme that they name: `candidates`: each row names 4 different clusters; among the test examples of one device no cluster is named by more than 4 of them. `owner`: each cluster is named exactly once. `cluster_sizes`: some cluster is full.
All inputs are finite; a program needn't handle non-finite values.
Results may differ from the reference program's by a relative error of at most 0.0003.
Values may be sent and summed in bfloat16 or wider, within the bound.
A program may use at most 128 MiB of HBM per device.

```python
import math
import jax
import jax.numpy as jnp
import numpy as np
from jax import lax

K = 8192
CAP = 768
TEST_DEV = 16
TOPC = 4
MOST = 4
NCLUS = 16
NTEST = 256
NTRAIN = 12288


def draw_test_grads(key, part):
    key = jax.random.fold_in(key, 11)
    first, second = jax.random.split(key, 2)
    base = jax.random.normal(first, (NTEST, K), jnp.float32)
    spread = jnp.exp(jax.random.uniform(second, (NTEST, 1), jnp.float32) * math.log(10.0))
    return (base * spread).astype(jnp.bfloat16)


def draw_train_grads(key, part):
    key = jax.random.fold_in(key, 13)
    first, second = jax.random.split(key, 2)
    base = jax.random.normal(first, (NTRAIN, K), jnp.float32)
    spread = jnp.exp(jax.random.uniform(second, (NTRAIN, 1), jnp.float32) * math.log(10.0))
    return (base * spread).astype(jnp.bfloat16)


def draw_cluster_sizes(key, part):
    key = jax.random.fold_in(key, 17)
    first, second = jax.random.split(key)
    sizes = jax.random.randint(first, (NCLUS,), CAP // 2, CAP + 1, jnp.int32)
    fullest = jax.random.randint(second, (), 0, NCLUS, jnp.int32)
    return jnp.where(jnp.arange(NCLUS, dtype=jnp.int32) == fullest, jnp.int32(CAP), sizes)


def assign_block(key, own, number, rows, count, top, limit, skew):
    ranking = jax.random.permutation(key, count)
    packed, common = shares(count, rows * top, limit, skew, True), shares(count, rows * top, limit, skew, False)
    places = jnp.arange(count)

    def named(sizes, rotation):
        used = int((sizes > 0).sum())
        fixed = max(1, used // 4)
        passed = fixed + (places - fixed + rotation * (used - fixed)) % max(1, count - fixed)
        return jnp.zeros((count,), jnp.int32).at[ranking[jnp.where(places < fixed, places, passed)]].set(jnp.asarray(sizes, jnp.int32))

    sizes = jnp.where(number % 4 == 0, named(packed, number // 4), named(common, number - number // 4 - 1))
    mixed = jax.random.permutation(jax.random.fold_in(own, 3), count)
    donor, taker = mixed[0:count // 2 * 2:2], mixed[1:count // 2 * 2:2]
    margin = jnp.minimum(sizes[donor] - 1, limit - sizes[taker]) // 2
    margin = jnp.where((donor == ranking[0]) | (taker == ranking[0]) | (sizes[taker] == 0), 0, jnp.maximum(margin, 0))
    passed = jax.random.randint(jax.random.fold_in(own, 4), (count // 2,), 0, 1 << 20) % (margin + 1)
    sizes = sizes.at[donor].add(-passed).at[taker].add(passed)
    members = jnp.searchsorted(jnp.cumsum(sizes), jnp.arange(rows * top), side="right").astype(jnp.int32)
    table = members.reshape(top, rows).T
    table = table[jax.random.permutation(jax.random.fold_in(own, 1), rows)]
    rotation = jax.random.randint(jax.random.fold_in(own, 2), (rows, 1), 0, top)
    return jnp.take_along_axis(table, (jnp.arange(top)[None, :] + rotation) % top, axis=1)


def shares(amount, total, reach, skew, full):
    loads = [(1 << 20) // math.isqrt(standing ** skew) + 1 for standing in range(1, amount + 1)]
    largest = reach if full else min(reach, max(-(-total // amount), total * loads[0] // sum(loads)))
    least = 1 if total - largest >= amount - 1 else 0
    counts, surplus = [largest] + [least] * (amount - 1), total - largest - least * (amount - 1)
    while surplus > 0:
        movable = [i for i in range(1, amount) if counts[i] < largest] or [i for i in range(1, amount) if counts[i] < reach]
        mass, budget = sum([loads[i] for i in movable]), surplus
        for i in movable:
            more = min(reach - counts[i], max(1, budget * loads[i] // mass), surplus)
            counts[i] = counts[i] + more
            surplus = surplus - more
    return np.array(counts)


def setup_inputs(seed: int = 0, part: int = 0) -> dict:
    key_of = jax.random.split(jax.random.key(seed), 6)
    part_keys = jax.random.split(jax.random.fold_in(key_of[5], part), 6)
    test_grads = draw_test_grads(jax.random.fold_in(jax.random.fold_in(key_of[5], part), 71), part)
    train_grads = draw_train_grads(jax.random.fold_in(jax.random.fold_in(key_of[5], part), 71), part)
    candidates_keys = jax.random.split(jax.random.fold_in(part_keys[2], 1), NTEST // TEST_DEV)
    candidates_turns = jax.random.permutation(jax.random.fold_in(part_keys[2], 3), NTEST // TEST_DEV)
    candidates = jax.vmap(lambda own, number: assign_block(jax.random.fold_in(part_keys[2], 2), own, number, TEST_DEV, NCLUS, TOPC, MOST, 2))(candidates_keys, candidates_turns).reshape((NTEST, TOPC))
    owner = jax.random.permutation(part_keys[3], NCLUS).astype(jnp.int32)
    cluster_sizes = draw_cluster_sizes(jax.random.fold_in(jax.random.fold_in(key_of[5], part), 71), part)
    return {"test_grads": test_grads, "train_grads": train_grads, "candidates": candidates, "owner": owner, "cluster_sizes": cluster_sizes}


EPS = 1e-06

def row_rms(cluster_rows):
    widened = cluster_rows.astype(jnp.float32)
    return jnp.sqrt(lax.optimization_barrier(jnp.mean(widened * widened, axis=1)) + EPS)

def reference(test_grads, train_grads, candidates, owner, cluster_sizes):
    stacked = train_grads.reshape(NCLUS, CAP, K)
    rms_table = lax.map(row_rms, stacked)
    positions = jnp.arange(CAP, dtype=jnp.int32)

    def one_test(inputs):
        query, chosen = inputs

        def one_pick(cluster):
            holder = owner[cluster].astype(jnp.int32)
            block = lax.dynamic_index_in_dim(stacked, holder, 0, keepdims=False)
            raw_dot = jnp.dot(block, query, preferred_element_type=jnp.float32)
            divided = raw_dot / rms_table[holder]
            return jnp.where(positions < cluster_sizes[cluster], divided, jnp.zeros_like(divided))
        return jax.vmap(one_pick)(chosen)
    scores = lax.map(one_test, (test_grads, candidates))
    valid_count = lax.optimization_barrier(jnp.sum(cluster_sizes[candidates], axis=1)).astype(jnp.float32)
    meansq = lax.optimization_barrier(jnp.sum(scores * scores, axis=(1, 2))) / valid_count
    return scores / jnp.sqrt(meansq + EPS)[:, None, None]
```

```python
import functools

import jax
import jax.numpy as jnp
from jax import lax
from jax.experimental import pallas as pl
from jax.experimental.pallas import tpu as pltpu
from jax.sharding import PartitionSpec as P

EPS = 1e-06
CHUNKS = 4
TILE = 16
F32 = jnp.float32
BF16 = jnp.bfloat16


def iota(shape, dim):
    return lax.broadcasted_iota(jnp.int32, shape, dim)


def dot_nn(a, b):
    return lax.dot_general(a, b, (((1,), (0,)), ((), ())), preferred_element_type=F32)


def dot_nt(a, b):
    return lax.dot_general(a, b, (((1,), (1,)), ((), ())), preferred_element_type=F32)


def log2(n):
    assert n & (n - 1) == 0
    return n.bit_length() - 1


def onehot(condition):
    return jnp.where(condition, 1.0, 0.0).astype(BF16)


def kernel(
    peers,
    slots,
    test_ref,
    train_ref,
    cand_ref,
    owner_ref,
    size_ref,
    out_ref,
    train_v,
    send_v,
    recv_v,
    square_v,
    score_v,
    answer_v,
    back_v,
    train_sem,
    send_sem,
    recv_sem,
    answer_sem,
    back_sem,
):
    tests, per_test = cand_ref.shape
    clusters = owner_ref.shape[1]
    chunks, capacity, chunk_width = train_v.shape
    subs = TILE // slots
    width = chunk_width // subs
    half = capacity // 2
    me = lax.axis_index("shard")

    def load(c):
        return pltpu.make_async_copy(
            train_ref.at[:, pl.ds(c * chunk_width, chunk_width)], train_v.at[c], train_sem.at[c]
        )

    def scatter(c, off):
        to = lax.rem(me + off, peers)
        return pltpu.make_async_remote_copy(
            src_ref=send_v.at[c, to],
            dst_ref=recv_v.at[c, me],
            send_sem=send_sem.at[c, off],
            recv_sem=recv_sem.at[c, off],
            device_id={"shard": to},
            device_id_type=pl.DeviceIdType.MESH,
        )

    def reply(off):
        to = lax.rem(me + off, peers)
        return pltpu.make_async_remote_copy(
            src_ref=answer_v.at[to],
            dst_ref=back_v.at[me],
            send_sem=answer_sem.at[off],
            recv_sem=back_sem.at[off],
            device_id={"shard": to},
            device_id_type=pl.DeviceIdType.MESH,
        )

    for c in range(chunks):
        load(c).start()

    barrier = pltpu.get_barrier_semaphore()

    @pl.loop(1, peers)
    def _(off):
        pl.semaphore_signal(
            barrier,
            inc=1,
            device_id={"shard": lax.rem(me + off, peers)},
            device_id_type=pl.DeviceIdType.MESH,
        )

    named = [
        onehot(cand_ref[:, j : j + 1] == iota((tests, clusters), 1)) for j in range(per_test)
    ]
    owned = onehot(owner_ref[...] == iota((peers, clusters), 0))
    holder = [dot_nt(chosen, owned) for chosen in named]
    asks = functools.reduce(jnp.add, holder)
    before = onehot(iota((tests, tests), 1) < iota((tests, tests), 0))
    place = dot_nn(before, asks.astype(BF16)) + 1.0
    taken = (asks * place).astype(BF16)

    rows = peers * TILE
    spread = onehot((iota((rows, peers), 0) >> log2(TILE)) == iota((rows, peers), 1))
    tile = onehot((iota((tests, subs * tests), 1) & (tests - 1)) == iota((tests, subs * tests), 0))
    wanted = dot_nn(dot_nt(spread, taken).astype(BF16), tile)
    row = iota((rows, subs * tests), 0) & (TILE - 1)
    column = iota((rows, subs * tests), 1)
    same_block = (row >> log2(slots)) == (column >> log2(tests))
    pick = onehot(same_block & (wanted == ((row & (slots - 1)) + 1).astype(F32)))

    for c in range(chunks):
        blocks = [
            test_ref[:, c * chunk_width + q * width : c * chunk_width + (q + 1) * width]
            for q in range(subs)
        ]
        block = dot_nn(pick, jnp.concatenate(blocks, axis=0)).astype(BF16)
        send_v[c] = block.reshape(peers, TILE, width)

    pl.semaphore_wait(barrier, peers - 1)

    for c in range(chunks):

        @pl.loop(1, peers)
        def _(off):
            scatter(c, off).start()

        recv_v[c, me] = send_v[c, me]

    step = 64
    square_v[...] = jnp.zeros_like(square_v)

    @pl.loop(0, chunks)
    def _(c):
        load(c).wait()

        @pl.loop(0, capacity // step)
        def _(b):
            at = pl.ds(pl.multiple_of(b * step, step), step)
            total = square_v[at, :]
            for k in range(chunk_width // 128):
                x = train_v[c, at, k * 128 : (k + 1) * 128].astype(F32)
                total += x * x
            square_v[at, :] = total

    mean = jnp.sum(square_v[...].T, axis=0, keepdims=True) / (chunks * chunk_width)
    mine = jnp.where(owner_ref[...] == me, size_ref[...], 0)
    my_size = jnp.sum(mine.astype(F32), axis=1, keepdims=True)
    live = iota((1, capacity), 1).astype(F32) < my_size
    scale = lax.rsqrt(mean + EPS)

    @pl.loop(0, chunks)
    def _(c):
        @pl.loop(1, peers)
        def _(off):
            scatter(c, off).wait_recv()

        got = recv_v[c].reshape(rows, width)
        which = (iota((rows, width), 0) & (TILE - 1)) >> log2(slots)
        spaced = jnp.concatenate(
            [jnp.where(which == q, got, jnp.zeros_like(got)) for q in range(subs)], axis=1
        )
        part = dot_nt(spaced, train_v[c])

        @pl.when(c == 0)
        def _():
            score_v[...] = part

        @pl.when(c != 0)
        def _():
            score_v[...] += part

    full = score_v[...].reshape(peers, 2, 8, capacity)
    full = (full[:, 0] + full[:, 1]).reshape(peers * 8, capacity)
    turn = slots
    shifted = iota((peers * 8, capacity), 0) & 7
    while turn < 8:
        ahead = pltpu.roll(full, peers * 8 - turn, 0)
        behind = pltpu.roll(full, turn, 0)
        full = full + jnp.where((shifted & turn) == 0, ahead, behind)
        turn *= 2
    full = jnp.where(live, full * scale, 0.0)
    sub = iota((peers * 8, half), 0) & 7
    packed = jnp.where(sub < 4, full[:, :half], full[:, half:])
    answer_v[...] = packed.reshape(peers, 8, half)

    @pl.loop(1, peers)
    def _(off):
        reply(off).start()

    back_v[me] = answer_v[me]

    wide = peers * 8
    spread_back = onehot((iota((wide, peers), 0) >> 3) == iota((wide, peers), 1))
    spot = iota((tests, wide), 1) & 7
    valid = jnp.zeros((tests, 1), F32)
    left, right = [], []
    for j in range(per_test):
        at = dot_nt((holder[j] * place).astype(BF16), spread_back)
        left.append(onehot(at == (spot + 1).astype(F32)))
        right.append(onehot(at == (spot - 3).astype(F32)))
        sizes = jnp.where(named[j] > 0, size_ref[...].astype(F32), 0.0)
        valid += jnp.sum(sizes, axis=1, keepdims=True)
    left = jnp.where(iota((per_test * tests, wide), 1) & 7 < 4, jnp.concatenate(left, axis=0), 0)
    right = jnp.where(
        iota((per_test * tests, wide), 1) & 7 >= 4, jnp.concatenate(right, axis=0), 0
    )
    select = jnp.concatenate([left, right], axis=0).astype(BF16)

    @pl.loop(1, peers)
    def _(off):
        reply(off).wait_recv()

    rest = back_v[...].reshape(wide, half)
    chosen = jnp.zeros((2 * per_test * tests, half), F32)
    for _ in range(3):
        term = rest.astype(BF16)
        chosen += dot_nn(select, term)
        rest = rest - term.astype(F32)

    entries = per_test * tests
    energy = jnp.zeros((tests, 1), F32)
    for j in range(per_test):
        for h in range(2):
            x = chosen[h * entries + j * tests : h * entries + (j + 1) * tests]
            energy += jnp.sum(x * x, axis=1, keepdims=True)
    factor = lax.rsqrt(energy / valid + EPS)
    for j in range(per_test):
        for h in range(2):
            x = chosen[h * entries + j * tests : h * entries + (j + 1) * tests]
            out_ref[:, j * capacity + h * half : j * capacity + (h + 1) * half] = x * factor

    @pl.loop(1, peers)
    def _(off):
        for c in range(chunks):
            scatter(c, off).wait_send()
        reply(off).wait_send()


def shards(test_grads, train_grads, candidates, owner, cluster_sizes):
    peers = lax.axis_size("shard")
    capacity, depth = train_grads.shape
    tests, per_test = candidates.shape
    slots = max(2, -(-tests * per_test // peers))
    subs = TILE // slots
    chunk = depth // CHUNKS
    half = capacity // 2
    vmem = pl.BlockSpec(memory_space=pltpu.VMEM)
    out = pl.pallas_call(
        functools.partial(kernel, peers, slots),
        out_shape=jax.ShapeDtypeStruct((tests, per_test * capacity), F32),
        in_specs=[vmem, pl.BlockSpec(memory_space=pl.ANY), vmem, vmem, vmem],
        out_specs=vmem,
        scratch_shapes=[
            pltpu.VMEM((CHUNKS, capacity, chunk), BF16),
            pltpu.VMEM((CHUNKS, peers, TILE, chunk // subs), BF16),
            pltpu.VMEM((CHUNKS, peers, TILE, chunk // subs), BF16),
            pltpu.VMEM((capacity, 128), F32),
            pltpu.VMEM((peers * TILE, capacity), F32),
            pltpu.VMEM((peers, 8, half), F32),
            pltpu.VMEM((peers, 8, half), F32),
            pltpu.SemaphoreType.DMA((CHUNKS,)),
            pltpu.SemaphoreType.DMA((CHUNKS, peers)),
            pltpu.SemaphoreType.DMA((CHUNKS, peers)),
            pltpu.SemaphoreType.DMA((peers,)),
            pltpu.SemaphoreType.DMA((peers,)),
        ],
        compiler_params=pltpu.CompilerParams(
            collective_id=0, has_side_effects=True, vmem_limit_bytes=56 * 1024 * 1024
        ),
    )(test_grads, train_grads, candidates, owner[None, :], cluster_sizes[None, :])
    return out.reshape(tests, per_test, capacity)


def solution(mesh):
    in_specs = (
        P(("groups", "shard"), None),
        P(("groups", "shard"), None),
        P(("groups", "shard"), None),
        P("groups"),
        P("groups"),
    )
    out_specs = P(("groups", "shard"), None, None)
    return jax.shard_map(shards, mesh=mesh, in_specs=in_specs, out_specs=out_specs, check_vma=False)
```

```python
import functools

import jax
import jax.numpy as jnp
from jax import lax
from jax.experimental import pallas as pl
from jax.experimental.pallas import tpu as pltpu
from jax.sharding import PartitionSpec as P

EPS = 1e-06
CHUNKS = 4
TILE = 16
SLAB = 4
F32 = jnp.float32
BF16 = jnp.bfloat16


def iota(shape, dim):
    return lax.broadcasted_iota(jnp.int32, shape, dim)


def dot_nn(a, b):
    return lax.dot_general(a, b, (((1,), (0,)), ((), ())), preferred_element_type=F32)


def dot_nt(a, b):
    return lax.dot_general(a, b, (((1,), (1,)), ((), ())), preferred_element_type=F32)


def log2(n):
    assert n & (n - 1) == 0
    return n.bit_length() - 1


def owner_wide(peers):
    return -(-peers // 128) * 128


def onehot(condition):
    return jnp.where(condition, 1.0, 0.0).astype(BF16)


def kernel(
    peers,
    slots,
    test_ref,
    train_ref,
    cand_ref,
    owner_ref,
    size_ref,
    out_ref,
    train_v,
    line_v,
    taken_v,
    pick_v,
    stage_v,
    recv_v,
    square_v,
    score_v,
    answer_v,
    back_v,
    train_sem,
    line_sem,
    down_sem,
    up_sem,
    taken_sem,
    told_sem,
    stage_sem,
    recv_sem,
    answer_sem,
    back_sem,
):
    per_test, tests = cand_ref.shape
    clusters = owner_ref.shape[1]
    chunks, capacity, chunk_width = train_v.shape
    subs = TILE // slots
    width = chunk_width // subs
    half = capacity // 2
    length = peers // SLAB
    me = lax.axis_index("shard")
    level = lax.div(me, SLAB)
    member = lax.rem(me, SLAB)
    rows = SLAB * TILE

    def remote(src, dst, sent, got, to):
        return pltpu.make_async_remote_copy(
            src_ref=src,
            dst_ref=dst,
            send_sem=sent,
            recv_sem=got,
            device_id={"shard": to},
            device_id_type=pl.DeviceIdType.MESH,
        )

    def load(c):
        return pltpu.make_async_copy(
            train_ref.at[:, pl.ds(c * chunk_width, chunk_width)], train_v.at[c], train_sem.at[c]
        )

    def down(s, c):
        at = line_v.at[s, c]
        return remote(at, at, down_sem.at[s, c], line_sem.at[s, c], lax.rem(me - SLAB + peers, peers))

    def up(s, c):
        at = line_v.at[s, c]
        return remote(at, at, up_sem.at[s, c], line_sem.at[s, c], lax.rem(me + SLAB, peers))

    def tell(off):
        to = lax.rem(me + off * SLAB, peers)
        at = taken_v.at[level]
        return remote(at, at, taken_sem.at[off], told_sem.at[level], to)

    def told(s):
        at = taken_v.at[s]
        return remote(at, at, taken_sem.at[0], told_sem.at[s], lax.rem(me + SLAB, peers))

    def hand(s, c, off):
        to = lax.rem(member + off, SLAB)
        return remote(
            stage_v.at[s, c, to],
            recv_v.at[s, c, member],
            stage_sem.at[s, c, off],
            recv_sem.at[s, c, off],
            level * SLAB + to,
        )

    def reply(s, g):
        to = s * SLAB + g
        return remote(answer_v.at[s, g], back_v.at[me], answer_sem.at[to], back_sem.at[me], to)

    def came(p):
        at = back_v.at[p]
        return remote(at, at, answer_sem.at[p], back_sem.at[p], lax.rem(me + 1, peers))

    for c in range(chunks):
        load(c).start()

    barrier = pltpu.get_barrier_semaphore()

    @pl.loop(1, peers)
    def _(off):
        pl.semaphore_signal(
            barrier,
            inc=1,
            device_id={"shard": lax.rem(me + off, peers)},
            device_id_type=pl.DeviceIdType.MESH,
        )

    for c in range(chunks):
        line_v[level, c] = test_ref[:, c * chunk_width : (c + 1) * chunk_width]

    eye = onehot(iota((tests, tests), 0) == iota((tests, tests), 1))
    cand = dot_nt(eye, cand_ref[...].astype(F32).astype(BF16))
    ids = iota((tests, clusters), 1).astype(F32)
    named = [onehot(cand[:, j : j + 1] == ids) for j in range(per_test)]
    owned = onehot(owner_ref[...] == iota((owner_wide(peers), clusters), 0))
    holder = [dot_nt(chosen, owned) for chosen in named]
    asks = functools.reduce(jnp.add, holder)
    before = onehot(iota((tests, tests), 1) < iota((tests, tests), 0))
    place = dot_nn(before, asks.astype(BF16)) + 1.0
    taken_v[level] = (asks * place).astype(BF16)

    def choose(s):
        wide = owner_wide(peers)
        spread = onehot(
            (iota((rows, wide), 0) >> log2(TILE)) + level * SLAB == iota((rows, wide), 1)
        )
        tile = onehot(
            (iota((tests, subs * tests), 1) & (tests - 1)) == iota((tests, subs * tests), 0)
        )
        wanted = dot_nn(dot_nt(spread, taken_v[s]).astype(BF16), tile)
        row = iota((rows, subs * tests), 0) & (TILE - 1)
        column = iota((rows, subs * tests), 1)
        same_block = (row >> log2(slots)) == (column >> log2(tests))
        return onehot(same_block & (wanted == ((row & (slots - 1)) + 1).astype(F32)))

    def deal(s, c, pick):
        blocks = [line_v[s, c, :, q * width : (q + 1) * width] for q in range(subs)]
        block = dot_nn(pick, jnp.concatenate(blocks, axis=0)).astype(BF16)
        stage_v[s, c] = block.reshape(SLAB, TILE, width)
        for off in range(1, SLAB):
            hand(s, c, off).start()
        recv_v[s, c, member] = stage_v[s, c, member]

    pl.semaphore_wait(barrier, peers - 1)

    @pl.loop(0, chunks)
    def _(c):
        @pl.when(level > 0)
        def _():
            down(level, c).start()

        @pl.when(level < length - 1)
        def _():
            up(level, c).start()

    @pl.loop(1, length)
    def _(off):
        tell(off).start()

    pick_v[0] = choose(level)

    @pl.loop(0, chunks)
    def _(c):
        deal(level, c, pick_v[0])

    step = 64
    square_v[...] = jnp.zeros_like(square_v)

    @pl.loop(0, chunks)
    def _(c):
        load(c).wait()

        @pl.loop(0, capacity // step)
        def _(b):
            at = pl.ds(pl.multiple_of(b * step, step), step)
            total = square_v[at, :]
            for k in range(chunk_width // 128):
                x = train_v[c, at, k * 128 : (k + 1) * 128].astype(F32)
                total += x * x
            square_v[at, :] = total

    mean = jnp.sum(square_v[...].T, axis=0, keepdims=True) / (chunks * chunk_width)
    mine = jnp.where(owner_ref[...] == me, size_ref[...], 0)
    my_size = jnp.sum(mine.astype(F32), axis=1, keepdims=True)
    live = iota((1, capacity), 1).astype(F32) < my_size
    scale = lax.rsqrt(mean + EPS)

    def multiply(s, c, way):
        for off in range(1, SLAB):
            hand(s, c, off).wait_recv()
        got = recv_v[s, c].reshape(rows, width)
        which = (iota((rows, width), 0) & (TILE - 1)) >> log2(slots)
        spaced = jnp.concatenate(
            [jnp.where(which == q, got, jnp.zeros_like(got)) for q in range(subs)], axis=1
        )
        part = dot_nt(spaced, train_v[c])

        @pl.when(c == 0)
        def _():
            score_v[way] = part

        @pl.when(c != 0)
        def _():
            score_v[way] += part

        @pl.when(c == chunks - 1)
        def _():
            answer(s, way)

    def answer(s, way):
        full = score_v[way].reshape(SLAB, 2, 8, capacity)
        full = (full[:, 0] + full[:, 1]).reshape(SLAB * 8, capacity)
        turn = slots
        at = iota((SLAB * 8, capacity), 0) & 7
        while turn < 8:
            ahead = pltpu.roll(full, SLAB * 8 - turn, 0)
            behind = pltpu.roll(full, turn, 0)
            full = full + jnp.where((at & turn) == 0, ahead, behind)
            turn *= 2
        full = jnp.where(live, full * scale, 0.0)
        sub = iota((SLAB * 8, half), 0) & 7
        packed = jnp.where(sub < 4, full[:, :half], full[:, half:])
        answer_v[s] = packed.reshape(SLAB, 8, half)
        for g in range(SLAB):

            @pl.when(s * SLAB + g != me)
            def _():
                reply(s, g).start()

        @pl.when(s == level)
        def _():
            back_v[me] = answer_v[s, member]

    @pl.loop(0, length * chunks + 1)
    def _(t):
        far, c = lax.div(t, chunks), lax.rem(t, chunks)
        for way in range(2):
            s = level - far if way else level + far
            there = (far > 0) & (far < length) & (s >= 0) & (s < length)

            @pl.when(there)
            def _():
                if way:
                    up(s, c).wait_recv()

                    @pl.when(level < length - 1)
                    def _():
                        up(s, c).start()

                else:
                    down(s, c).wait_recv()

                    @pl.when(level > 0)
                    def _():
                        down(s, c).start()

                @pl.when(c == 0)
                def _():
                    told(s).wait_recv()
                    pick_v[way] = choose(s)

                deal(s, c, pick_v[way])

        last = t - 1
        far, c = lax.div(last + chunks, chunks) - 1, lax.rem(last + chunks, chunks)
        for way in range(2):
            s = level - far if way else level + far
            there = (t > 0) & (s >= 0) & (s < length)
            if way:
                there = there & (far > 0)

            @pl.when(there)
            def _():
                multiply(s, c, way)

    wide = peers * 8
    spread_back = onehot(
        (iota((wide, owner_wide(peers)), 0) >> 3) == iota((wide, owner_wide(peers)), 1)
    )
    spot = iota((tests, wide), 1) & 7
    valid = jnp.zeros((tests, 1), F32)
    left, right = [], []
    for j in range(per_test):
        at = dot_nt((holder[j] * place).astype(BF16), spread_back)
        left.append(onehot(at == (spot + 1).astype(F32)))
        right.append(onehot(at == (spot - 3).astype(F32)))
        sizes = jnp.where(named[j] > 0, size_ref[...].astype(F32), 0.0)
        valid += jnp.sum(sizes, axis=1, keepdims=True)
    left = jnp.where(iota((per_test * tests, wide), 1) & 7 < 4, jnp.concatenate(left, axis=0), 0)
    right = jnp.where(
        iota((per_test * tests, wide), 1) & 7 >= 4, jnp.concatenate(right, axis=0), 0
    )
    select = jnp.concatenate([left, right], axis=0).astype(BF16)

    @pl.loop(1, peers)
    def _(off):
        came(lax.rem(me + off, peers)).wait_recv()

    rest = back_v[...].reshape(wide, half)
    chosen = jnp.zeros((2 * per_test * tests, half), F32)
    for _ in range(3):
        term = rest.astype(BF16)
        chosen += dot_nn(select, term)
        rest = rest - term.astype(F32)

    entries = per_test * tests
    energy = jnp.zeros((tests, 1), F32)
    for j in range(per_test):
        for h in range(2):
            x = chosen[h * entries + j * tests : h * entries + (j + 1) * tests]
            energy += jnp.sum(x * x, axis=1, keepdims=True)
    factor = lax.rsqrt(energy / valid + EPS)
    for j in range(per_test):
        for h in range(2):
            x = chosen[h * entries + j * tests : h * entries + (j + 1) * tests]
            out_ref[:, j, h * half : (h + 1) * half] = x * factor

    @pl.loop(0, length)
    def _(s):
        @pl.loop(0, chunks)
        def _(c):
            @pl.when((level > 0) & (s >= level))
            def _():
                down(s, c).wait_send()

            @pl.when((level < length - 1) & (s <= level))
            def _():
                up(s, c).wait_send()

            for off in range(1, SLAB):
                hand(s, c, off).wait_send()

        for g in range(SLAB):

            @pl.when(s * SLAB + g != me)
            def _():
                reply(s, g).wait_send()

    @pl.loop(1, length)
    def _(off):
        tell(off).wait_send()


def shards(test_grads, train_grads, candidates, owner, cluster_sizes):
    peers = lax.axis_size("shard")
    capacity, depth = train_grads.shape
    tests, per_test = candidates.shape
    slots = max(2, -(-tests * per_test // peers))
    subs = TILE // slots
    chunk = depth // CHUNKS
    half = capacity // 2
    length = peers // SLAB
    vmem = pl.BlockSpec(memory_space=pltpu.VMEM)
    out = pl.pallas_call(
        functools.partial(kernel, peers, slots),
        out_shape=jax.ShapeDtypeStruct((tests, per_test, capacity), F32),
        in_specs=[vmem, pl.BlockSpec(memory_space=pl.ANY), vmem, vmem, vmem],
        out_specs=vmem,
        scratch_shapes=[
            pltpu.VMEM((CHUNKS, capacity, chunk), BF16),
            pltpu.VMEM((length, CHUNKS, tests, chunk), BF16),
            pltpu.VMEM((length, tests, owner_wide(peers)), BF16),
            pltpu.VMEM((2, SLAB * TILE, subs * tests), BF16),
            pltpu.VMEM((length, CHUNKS, SLAB, TILE, chunk // subs), BF16),
            pltpu.VMEM((length, CHUNKS, SLAB, TILE, chunk // subs), BF16),
            pltpu.VMEM((capacity, 128), F32),
            pltpu.VMEM((2, SLAB * TILE, capacity), F32),
            pltpu.VMEM((length, SLAB, 8, half), F32),
            pltpu.VMEM((peers, 8, half), F32),
            pltpu.SemaphoreType.DMA((CHUNKS,)),
            pltpu.SemaphoreType.DMA((length, CHUNKS)),
            pltpu.SemaphoreType.DMA((length, CHUNKS)),
            pltpu.SemaphoreType.DMA((length, CHUNKS)),
            pltpu.SemaphoreType.DMA((length,)),
            pltpu.SemaphoreType.DMA((length,)),
            pltpu.SemaphoreType.DMA((length, CHUNKS, SLAB)),
            pltpu.SemaphoreType.DMA((length, CHUNKS, SLAB)),
            pltpu.SemaphoreType.DMA((peers,)),
            pltpu.SemaphoreType.DMA((peers,)),
        ],
        compiler_params=pltpu.CompilerParams(
            collective_id=0, has_side_effects=True, vmem_limit_bytes=56 * 1024 * 1024
        ),
    )(test_grads, train_grads, candidates.T, owner[None, :], cluster_sizes[None, :])
    return out


def solution(mesh):
    in_specs = (
        P(("groups", "shard"), None),
        P(("groups", "shard"), None),
        P(("groups", "shard"), None),
        P("groups"),
        P("groups"),
    )
    out_specs = P(("groups", "shard"), None, None)
    return jax.shard_map(shards, mesh=mesh, in_specs=in_specs, out_specs=out_specs, check_vma=False)
```

```python
import functools

import jax
import jax.numpy as jnp
from jax import lax
from jax.experimental import pallas as pl
from jax.experimental.pallas import tpu as pltpu
from jax.sharding import PartitionSpec as P

EPS = 1e-06
CHUNKS = 4
TILE = 16
F32 = jnp.float32
BF16 = jnp.bfloat16


def iota(shape, dim):
    return lax.broadcasted_iota(jnp.int32, shape, dim)


def dot_nn(a, b):
    return lax.dot_general(a, b, (((1,), (0,)), ((), ())), preferred_element_type=F32)


def dot_nt(a, b):
    return lax.dot_general(a, b, (((1,), (1,)), ((), ())), preferred_element_type=F32)


def log2(n):
    assert n & (n - 1) == 0
    return n.bit_length() - 1


def onehot(condition):
    return jnp.where(condition, 1.0, 0.0).astype(BF16)


def kernel(
    peers,
    slots,
    test_ref,
    train_ref,
    cand_ref,
    owner_ref,
    size_ref,
    out_ref,
    train_v,
    send_v,
    recv_v,
    square_v,
    score_v,
    answer_v,
    back_v,
    train_sem,
    send_sem,
    recv_sem,
    answer_sem,
    back_sem,
):
    per_test, tests = cand_ref.shape
    clusters = owner_ref.shape[1]
    chunks, capacity, chunk_width = train_v.shape
    subs = TILE // slots
    width = chunk_width // subs
    half = capacity // 2
    me = lax.axis_index("shard")

    def load(c):
        return pltpu.make_async_copy(
            train_ref.at[:, pl.ds(c * chunk_width, chunk_width)], train_v.at[c], train_sem.at[c]
        )

    def scatter(c, off):
        to = lax.rem(me + off, peers)
        return pltpu.make_async_remote_copy(
            src_ref=send_v.at[c, to],
            dst_ref=recv_v.at[c, me],
            send_sem=send_sem.at[c, off],
            recv_sem=recv_sem.at[c, off],
            device_id={"shard": to},
            device_id_type=pl.DeviceIdType.MESH,
        )

    def reply(off):
        to = lax.rem(me + off, peers)
        return pltpu.make_async_remote_copy(
            src_ref=answer_v.at[to],
            dst_ref=back_v.at[me],
            send_sem=answer_sem.at[off],
            recv_sem=back_sem.at[off],
            device_id={"shard": to},
            device_id_type=pl.DeviceIdType.MESH,
        )

    for c in range(chunks):
        load(c).start()

    barrier = pltpu.get_barrier_semaphore()

    @pl.loop(1, peers)
    def _(off):
        pl.semaphore_signal(
            barrier,
            inc=1,
            device_id={"shard": lax.rem(me + off, peers)},
            device_id_type=pl.DeviceIdType.MESH,
        )

    eye = onehot(iota((tests, tests), 0) == iota((tests, tests), 1))
    cand = dot_nt(eye, cand_ref[...].astype(F32).astype(BF16))
    ids = iota((tests, clusters), 1).astype(F32)
    named = [onehot(cand[:, j : j + 1] == ids) for j in range(per_test)]
    owned = onehot(owner_ref[...] == iota((peers, clusters), 0))
    holder = [dot_nt(chosen, owned) for chosen in named]
    asks = functools.reduce(jnp.add, holder)
    before = onehot(iota((tests, tests), 1) < iota((tests, tests), 0))
    place = dot_nn(before, asks.astype(BF16)) + 1.0
    taken = (asks * place).astype(BF16)

    rows = peers * TILE
    spread = onehot((iota((rows, peers), 0) >> log2(TILE)) == iota((rows, peers), 1))
    tile = onehot((iota((tests, subs * tests), 1) & (tests - 1)) == iota((tests, subs * tests), 0))
    wanted = dot_nn(dot_nt(spread, taken).astype(BF16), tile)
    row = iota((rows, subs * tests), 0) & (TILE - 1)
    column = iota((rows, subs * tests), 1)
    same_block = (row >> log2(slots)) == (column >> log2(tests))
    pick = onehot(same_block & (wanted == ((row & (slots - 1)) + 1).astype(F32)))

    for c in range(chunks):
        blocks = [
            test_ref[:, c * chunk_width + q * width : c * chunk_width + (q + 1) * width]
            for q in range(subs)
        ]
        block = dot_nn(pick, jnp.concatenate(blocks, axis=0)).astype(BF16)
        send_v[c] = block.reshape(peers, TILE, width)

    pl.semaphore_wait(barrier, peers - 1)

    for c in range(chunks):

        @pl.loop(1, peers)
        def _(off):
            scatter(c, off).start()

        recv_v[c, me] = send_v[c, me]

    step = 64
    square_v[...] = jnp.zeros_like(square_v)

    @pl.loop(0, chunks)
    def _(c):
        load(c).wait()

        @pl.loop(0, capacity // step)
        def _(b):
            at = pl.ds(pl.multiple_of(b * step, step), step)
            total = square_v[at, :]
            for k in range(chunk_width // 128):
                x = train_v[c, at, k * 128 : (k + 1) * 128].astype(F32)
                total += x * x
            square_v[at, :] = total

    mean = jnp.sum(square_v[...].T, axis=0, keepdims=True) / (chunks * chunk_width)
    mine = jnp.where(owner_ref[...] == me, size_ref[...], 0)
    my_size = jnp.sum(mine.astype(F32), axis=1, keepdims=True)
    live = iota((1, capacity), 1).astype(F32) < my_size
    scale = lax.rsqrt(mean + EPS)

    @pl.loop(0, chunks)
    def _(c):
        @pl.loop(1, peers)
        def _(off):
            scatter(c, off).wait_recv()

        got = recv_v[c].reshape(rows, width)
        which = (iota((rows, width), 0) & (TILE - 1)) >> log2(slots)
        spaced = jnp.concatenate(
            [jnp.where(which == q, got, jnp.zeros_like(got)) for q in range(subs)], axis=1
        )
        part = dot_nt(spaced, train_v[c])

        @pl.when(c == 0)
        def _():
            score_v[...] = part

        @pl.when(c != 0)
        def _():
            score_v[...] += part

    full = score_v[...].reshape(peers, 2, 8, capacity)
    full = (full[:, 0] + full[:, 1]).reshape(peers * 8, capacity)
    turn = slots
    shifted = iota((peers * 8, capacity), 0) & 7
    while turn < 8:
        ahead = pltpu.roll(full, peers * 8 - turn, 0)
        behind = pltpu.roll(full, turn, 0)
        full = full + jnp.where((shifted & turn) == 0, ahead, behind)
        turn *= 2
    full = jnp.where(live, full * scale, 0.0)
    sub = iota((peers * 8, half), 0) & 7
    packed = jnp.where(sub < 4, full[:, :half], full[:, half:])
    answer_v[...] = packed.reshape(peers, 8, half)

    @pl.loop(1, peers)
    def _(off):
        reply(off).start()

    back_v[me] = answer_v[me]

    wide = peers * 8
    spread_back = onehot((iota((wide, peers), 0) >> 3) == iota((wide, peers), 1))
    spot = iota((tests, wide), 1) & 7
    valid = jnp.zeros((tests, 1), F32)
    left, right = [], []
    for j in range(per_test):
        at = dot_nt((holder[j] * place).astype(BF16), spread_back)
        left.append(onehot(at == (spot + 1).astype(F32)))
        right.append(onehot(at == (spot - 3).astype(F32)))
        sizes = jnp.where(named[j] > 0, size_ref[...].astype(F32), 0.0)
        valid += jnp.sum(sizes, axis=1, keepdims=True)
    left = jnp.where(iota((per_test * tests, wide), 1) & 7 < 4, jnp.concatenate(left, axis=0), 0)
    right = jnp.where(
        iota((per_test * tests, wide), 1) & 7 >= 4, jnp.concatenate(right, axis=0), 0
    )
    select = jnp.concatenate([left, right], axis=0).astype(BF16)

    @pl.loop(1, peers)
    def _(off):
        reply(off).wait_recv()

    rest = back_v[...].reshape(wide, half)
    chosen = jnp.zeros((2 * per_test * tests, half), F32)
    for _ in range(3):
        term = rest.astype(BF16)
        chosen += dot_nn(select, term)
        rest = rest - term.astype(F32)

    entries = per_test * tests
    energy = jnp.zeros((tests, 1), F32)
    for j in range(per_test):
        for h in range(2):
            x = chosen[h * entries + j * tests : h * entries + (j + 1) * tests]
            energy += jnp.sum(x * x, axis=1, keepdims=True)
    factor = lax.rsqrt(energy / valid + EPS)
    for j in range(per_test):
        for h in range(2):
            x = chosen[h * entries + j * tests : h * entries + (j + 1) * tests]
            out_ref[:, j, h * half : (h + 1) * half] = x * factor

    @pl.loop(1, peers)
    def _(off):
        for c in range(chunks):
            scatter(c, off).wait_send()
        reply(off).wait_send()


def shards(test_grads, train_grads, candidates, owner, cluster_sizes):
    peers = lax.axis_size("shard")
    capacity, depth = train_grads.shape
    tests, per_test = candidates.shape
    slots = max(2, -(-tests * per_test // peers))
    subs = TILE // slots
    chunk = depth // CHUNKS
    half = capacity // 2
    vmem = pl.BlockSpec(memory_space=pltpu.VMEM)
    out = pl.pallas_call(
        functools.partial(kernel, peers, slots),
        out_shape=jax.ShapeDtypeStruct((tests, per_test, capacity), F32),
        in_specs=[vmem, pl.BlockSpec(memory_space=pl.ANY), vmem, vmem, vmem],
        out_specs=vmem,
        scratch_shapes=[
            pltpu.VMEM((CHUNKS, capacity, chunk), BF16),
            pltpu.VMEM((CHUNKS, peers, TILE, chunk // subs), BF16),
            pltpu.VMEM((CHUNKS, peers, TILE, chunk // subs), BF16),
            pltpu.VMEM((capacity, 128), F32),
            pltpu.VMEM((peers * TILE, capacity), F32),
            pltpu.VMEM((peers, 8, half), F32),
            pltpu.VMEM((peers, 8, half), F32),
            pltpu.SemaphoreType.DMA((CHUNKS,)),
            pltpu.SemaphoreType.DMA((CHUNKS, peers)),
            pltpu.SemaphoreType.DMA((CHUNKS, peers)),
            pltpu.SemaphoreType.DMA((peers,)),
            pltpu.SemaphoreType.DMA((peers,)),
        ],
        compiler_params=pltpu.CompilerParams(
            collective_id=0, has_side_effects=True, vmem_limit_bytes=56 * 1024 * 1024
        ),
    )(test_grads, train_grads, candidates.T, owner[None, :], cluster_sizes[None, :])
    return out


def solution(mesh):
    in_specs = (
        P(("groups", "shard"), None),
        P(("groups", "shard"), None),
        P(("groups", "shard"), None),
        P("groups"),
        P("groups"),
    )
    out_specs = P(("groups", "shard"), None, None)
    return jax.shard_map(shards, mesh=mesh, in_specs=in_specs, out_specs=out_specs, check_vma=False)
```

```python
import functools

import jax
import jax.numpy as jnp
from jax import lax
from jax.experimental import pallas as pl
from jax.experimental.pallas import tpu as pltpu
from jax.sharding import PartitionSpec as P

EPS = 1e-06
CHUNKS = 4
TILE = 16
F32 = jnp.float32
BF16 = jnp.bfloat16


def iota(shape, dim):
    return lax.broadcasted_iota(jnp.int32, shape, dim)


def dot_nn(a, b):
    return lax.dot_general(a, b, (((1,), (0,)), ((), ())), preferred_element_type=F32)


def dot_nt(a, b):
    return lax.dot_general(a, b, (((1,), (1,)), ((), ())), preferred_element_type=F32)


def log2(n):
    assert n & (n - 1) == 0
    return n.bit_length() - 1


def padded(peers):
    return -(-peers // 128) * 128


def onehot(condition):
    return jnp.where(condition, 1.0, 0.0).astype(BF16)


def kernel(
    peers,
    slots,
    test_ref,
    train_ref,
    cand_ref,
    owner_ref,
    size_ref,
    out_ref,
    train_v,
    far_v,
    taken_v,
    send_v,
    relay_v,
    recv_v,
    square_v,
    score_v,
    answer_v,
    back_v,
    train_sem,
    raw_sem,
    far_sem,
    taken_sem,
    told_sem,
    send_sem,
    recv_sem,
    answer_sem,
    back_sem,
):
    per_test, tests = cand_ref.shape
    clusters = owner_ref.shape[1]
    chunks, capacity, chunk_width = train_v.shape
    subs = TILE // slots
    width = chunk_width // subs
    half = capacity // 2
    wide_peers = padded(peers)
    me = lax.axis_index("shard")

    def load(c):
        return pltpu.make_async_copy(
            train_ref.at[:, pl.ds(c * chunk_width, chunk_width)], train_v.at[c], train_sem.at[c]
        )

    near = peers // 2
    base = lax.div(me, near) * near
    member = lax.rem(me, near)
    partner = lax.rem(me + near, peers)

    def deal(which, c, off):
        to = lax.rem(member + off, near)
        return pltpu.make_async_remote_copy(
            src_ref=(relay_v if which else send_v).at[c, to],
            dst_ref=recv_v.at[c, partner if which else me],
            send_sem=send_sem.at[which, c, off],
            recv_sem=recv_sem.at[which, c, off],
            device_id={"shard": base + to},
            device_id_type=pl.DeviceIdType.MESH,
        )

    def cross(c):
        return pltpu.make_async_remote_copy(
            src_ref=test_ref.at[:, pl.ds(c * chunk_width, chunk_width)],
            dst_ref=far_v.at[c],
            send_sem=raw_sem.at[c],
            recv_sem=far_sem.at[c],
            device_id={"shard": partner},
            device_id_type=pl.DeviceIdType.MESH,
        )

    def tell():
        return pltpu.make_async_remote_copy(
            src_ref=taken_v.at[0],
            dst_ref=taken_v.at[1],
            send_sem=taken_sem,
            recv_sem=told_sem,
            device_id={"shard": partner},
            device_id_type=pl.DeviceIdType.MESH,
        )

    def reply(off):
        to = lax.rem(me + off, peers)
        return pltpu.make_async_remote_copy(
            src_ref=answer_v.at[to],
            dst_ref=back_v.at[me],
            send_sem=answer_sem.at[off],
            recv_sem=back_sem.at[off],
            device_id={"shard": to},
            device_id_type=pl.DeviceIdType.MESH,
        )

    for c in range(chunks):
        load(c).start()

    barrier = pltpu.get_barrier_semaphore()

    @pl.loop(1, peers)
    def _(off):
        pl.semaphore_signal(
            barrier,
            inc=1,
            device_id={"shard": lax.rem(me + off, peers)},
            device_id_type=pl.DeviceIdType.MESH,
        )

    eye = onehot(iota((tests, tests), 0) == iota((tests, tests), 1))
    cand = dot_nt(eye, cand_ref[...].astype(F32).astype(BF16))
    ids = iota((tests, clusters), 1).astype(F32)
    named = [onehot(cand[:, j : j + 1] == ids) for j in range(per_test)]
    owned = onehot(owner_ref[...] == iota((wide_peers, clusters), 0))
    holder = [dot_nt(chosen, owned) for chosen in named]
    asks = functools.reduce(jnp.add, holder)
    before = onehot(iota((tests, tests), 1) < iota((tests, tests), 0))
    place = dot_nn(before, asks.astype(BF16)) + 1.0
    taken_v[0] = (asks * place).astype(BF16)

    dealt = near * TILE

    def choose(taken):
        spread = onehot(
            (iota((dealt, wide_peers), 0) >> log2(TILE)) + base == iota((dealt, wide_peers), 1)
        )
        tile = onehot(
            (iota((tests, subs * tests), 1) & (tests - 1)) == iota((tests, subs * tests), 0)
        )
        wanted = dot_nn(dot_nt(spread, taken).astype(BF16), tile)
        row = iota((dealt, subs * tests), 0) & (TILE - 1)
        column = iota((dealt, subs * tests), 1)
        same_block = (row >> log2(slots)) == (column >> log2(tests))
        return onehot(same_block & (wanted == ((row & (slots - 1)) + 1).astype(F32)))

    def select_rows(pick, chunk):
        blocks = [chunk[:, q * width : (q + 1) * width] for q in range(subs)]
        block = dot_nn(pick, jnp.concatenate(blocks, axis=0)).astype(BF16)
        return block.reshape(near, TILE, width)

    pick = choose(taken_v[0])
    for c in range(chunks):
        send_v[c] = select_rows(pick, test_ref[:, c * chunk_width : (c + 1) * chunk_width])

    pl.semaphore_wait(barrier, peers - 1)

    tell().start()
    for c in range(chunks):
        cross(c).start()
    for c in range(chunks):

        @pl.loop(1, near)
        def _(off):
            deal(0, c, off).start()

        recv_v[c, me] = send_v[c, member]

    tell().wait_recv()
    pick = choose(taken_v[1])
    square_v[...] = jnp.zeros_like(square_v)
    step = 64

    for c in range(chunks):
        cross(c).wait_recv()
        relay_v[c] = select_rows(pick, far_v[c])

        @pl.loop(1, near)
        def _(off):
            deal(1, c, off).start()

        recv_v[c, partner] = relay_v[c, member]
        load(c).wait()

        @pl.loop(0, capacity // step)
        def _(b):
            at = pl.ds(pl.multiple_of(b * step, step), step)
            total = square_v[at, :]
            for k in range(chunk_width // 128):
                x = train_v[c, at, k * 128 : (k + 1) * 128].astype(F32)
                total += x * x
            square_v[at, :] = total

    mean = jnp.sum(square_v[...].T, axis=0, keepdims=True) / (chunks * chunk_width)
    mine = jnp.where(owner_ref[...] == me, size_ref[...], 0)
    my_size = jnp.sum(mine.astype(F32), axis=1, keepdims=True)
    live = iota((1, capacity), 1).astype(F32) < my_size
    scale = lax.rsqrt(mean + EPS)

    @pl.loop(0, chunks)
    def _(c):
        @pl.loop(1, near)
        def _(off):
            deal(0, c, off).wait_recv()
            deal(1, c, off).wait_recv()

        rows = peers * TILE
        got = recv_v[c].reshape(rows, width)
        which = (iota((rows, width), 0) & (TILE - 1)) >> log2(slots)
        spaced = jnp.concatenate(
            [jnp.where(which == q, got, jnp.zeros_like(got)) for q in range(subs)], axis=1
        )
        part = dot_nt(spaced, train_v[c])

        @pl.when(c == 0)
        def _():
            score_v[...] = part

        @pl.when(c != 0)
        def _():
            score_v[...] += part

    full = score_v[...].reshape(peers, 2, 8, capacity)
    full = (full[:, 0] + full[:, 1]).reshape(peers * 8, capacity)
    turn = slots
    shifted = iota((peers * 8, capacity), 0) & 7
    while turn < 8:
        ahead = pltpu.roll(full, peers * 8 - turn, 0)
        behind = pltpu.roll(full, turn, 0)
        full = full + jnp.where((shifted & turn) == 0, ahead, behind)
        turn *= 2
    full = jnp.where(live, full * scale, 0.0)
    sub = iota((peers * 8, half), 0) & 7
    packed = jnp.where(sub < 4, full[:, :half], full[:, half:])
    answer_v[...] = packed.reshape(peers, 8, half)

    @pl.loop(1, peers)
    def _(off):
        reply(off).start()

    back_v[me] = answer_v[me]

    wide = peers * 8
    spread_back = onehot(
        (iota((wide, wide_peers), 0) >> 3) == iota((wide, wide_peers), 1)
    )
    spot = iota((tests, wide), 1) & 7
    valid = jnp.zeros((tests, 1), F32)
    left, right = [], []
    for j in range(per_test):
        at = dot_nt((holder[j] * place).astype(BF16), spread_back)
        left.append(onehot(at == (spot + 1).astype(F32)))
        right.append(onehot(at == (spot - 3).astype(F32)))
        sizes = jnp.where(named[j] > 0, size_ref[...].astype(F32), 0.0)
        valid += jnp.sum(sizes, axis=1, keepdims=True)
    left = jnp.where(iota((per_test * tests, wide), 1) & 7 < 4, jnp.concatenate(left, axis=0), 0)
    right = jnp.where(
        iota((per_test * tests, wide), 1) & 7 >= 4, jnp.concatenate(right, axis=0), 0
    )
    select = jnp.concatenate([left, right], axis=0).astype(BF16)

    @pl.loop(1, peers)
    def _(off):
        reply(off).wait_recv()

    rest = back_v[...].reshape(wide, half)
    chosen = jnp.zeros((2 * per_test * tests, half), F32)
    for _ in range(3):
        term = rest.astype(BF16)
        chosen += dot_nn(select, term)
        rest = rest - term.astype(F32)

    entries = per_test * tests
    energy = jnp.zeros((tests, 1), F32)
    for j in range(per_test):
        for h in range(2):
            x = chosen[h * entries + j * tests : h * entries + (j + 1) * tests]
            energy += jnp.sum(x * x, axis=1, keepdims=True)
    factor = lax.rsqrt(energy / valid + EPS)
    for j in range(per_test):
        for h in range(2):
            x = chosen[h * entries + j * tests : h * entries + (j + 1) * tests]
            out_ref[:, j, h * half : (h + 1) * half] = x * factor

    @pl.loop(1, peers)
    def _(off):
        reply(off).wait_send()

    @pl.loop(1, near)
    def _(off):
        for c in range(chunks):
            deal(0, c, off).wait_send()
            deal(1, c, off).wait_send()

    for c in range(chunks):
        cross(c).wait_send()
    tell().wait_send()


def shards(test_grads, train_grads, candidates, owner, cluster_sizes):
    peers = lax.axis_size("shard")
    capacity, depth = train_grads.shape
    tests, per_test = candidates.shape
    slots = max(2, -(-tests * per_test // peers))
    subs = TILE // slots
    chunk = depth // CHUNKS
    half = capacity // 2
    near = peers // 2
    vmem = pl.BlockSpec(memory_space=pltpu.VMEM)
    out = pl.pallas_call(
        functools.partial(kernel, peers, slots),
        out_shape=jax.ShapeDtypeStruct((tests, per_test, capacity), F32),
        in_specs=[vmem, pl.BlockSpec(memory_space=pl.ANY), vmem, vmem, vmem],
        out_specs=vmem,
        scratch_shapes=[
            pltpu.VMEM((CHUNKS, capacity, chunk), BF16),
            pltpu.VMEM((CHUNKS, tests, chunk), BF16),
            pltpu.VMEM((2, tests, padded(peers)), BF16),
            pltpu.VMEM((CHUNKS, near, TILE, chunk // subs), BF16),
            pltpu.VMEM((CHUNKS, near, TILE, chunk // subs), BF16),
            pltpu.VMEM((CHUNKS, peers, TILE, chunk // subs), BF16),
            pltpu.VMEM((capacity, 128), F32),
            pltpu.VMEM((peers * TILE, capacity), F32),
            pltpu.VMEM((peers, 8, half), F32),
            pltpu.VMEM((peers, 8, half), F32),
            pltpu.SemaphoreType.DMA((CHUNKS,)),
            pltpu.SemaphoreType.DMA((CHUNKS,)),
            pltpu.SemaphoreType.DMA((CHUNKS,)),
            pltpu.SemaphoreType.DMA,
            pltpu.SemaphoreType.DMA,
            pltpu.SemaphoreType.DMA((2, CHUNKS, near)),
            pltpu.SemaphoreType.DMA((2, CHUNKS, near)),
            pltpu.SemaphoreType.DMA((peers,)),
            pltpu.SemaphoreType.DMA((peers,)),
        ],
        compiler_params=pltpu.CompilerParams(
            collective_id=0, has_side_effects=True, vmem_limit_bytes=56 * 1024 * 1024
        ),
    )(test_grads, train_grads, candidates.T, owner[None, :], cluster_sizes[None, :])
    return out


def solution(mesh):
    in_specs = (
        P(("groups", "shard"), None),
        P(("groups", "shard"), None),
        P(("groups", "shard"), None),
        P("groups"),
        P("groups"),
    )
    out_specs = P(("groups", "shard"), None, None)
    return jax.shard_map(shards, mesh=mesh, in_specs=in_specs, out_specs=out_specs, check_vma=False)
```

```python
import functools

import jax
import jax.numpy as jnp
from jax import lax
from jax.experimental import pallas as pl
from jax.experimental.pallas import tpu as pltpu
from jax.sharding import PartitionSpec as P

EPS = 1e-06
CHUNKS = 8
TILE = 16
F32 = jnp.float32
BF16 = jnp.bfloat16


def iota(shape, dim):
    return lax.broadcasted_iota(jnp.int32, shape, dim)


def dot_nn(a, b):
    return lax.dot_general(a, b, (((1,), (0,)), ((), ())), preferred_element_type=F32)


def dot_nt(a, b):
    return lax.dot_general(a, b, (((1,), (1,)), ((), ())), preferred_element_type=F32)


def log2(n):
    assert n & (n - 1) == 0
    return n.bit_length() - 1


def padded(peers):
    return -(-peers // 128) * 128


def onehot(condition):
    return jnp.where(condition, 1.0, 0.0).astype(BF16)


def kernel(
    peers,
    slots,
    test_ref,
    train_ref,
    cand_ref,
    owner_ref,
    size_ref,
    out_ref,
    train_v,
    far_v,
    taken_v,
    send_v,
    relay_v,
    recv_v,
    square_v,
    score_v,
    answer_v,
    back_v,
    train_sem,
    raw_sem,
    far_sem,
    taken_sem,
    told_sem,
    send_sem,
    recv_sem,
    answer_sem,
    back_sem,
):
    per_test, tests = cand_ref.shape
    clusters = owner_ref.shape[1]
    chunks, capacity, chunk_width = train_v.shape
    subs = TILE // slots
    width = chunk_width // subs
    half = capacity // 2
    wide_peers = padded(peers)
    me = lax.axis_index("shard")

    def load(c):
        return pltpu.make_async_copy(
            train_ref.at[:, pl.ds(c * chunk_width, chunk_width)], train_v.at[c], train_sem.at[c]
        )

    near = peers // 2
    base = lax.div(me, near) * near
    member = lax.rem(me, near)
    partner = lax.rem(me + near, peers)

    def deal(which, c, off):
        to = lax.rem(member + off, near)
        return pltpu.make_async_remote_copy(
            src_ref=(relay_v if which else send_v).at[c, to],
            dst_ref=recv_v.at[c, partner if which else me],
            send_sem=send_sem.at[which, c, off],
            recv_sem=recv_sem.at[which, c, off],
            device_id={"shard": base + to},
            device_id_type=pl.DeviceIdType.MESH,
        )

    def cross(c):
        return pltpu.make_async_remote_copy(
            src_ref=test_ref.at[:, pl.ds(c * chunk_width, chunk_width)],
            dst_ref=far_v.at[c],
            send_sem=raw_sem.at[c],
            recv_sem=far_sem.at[c],
            device_id={"shard": partner},
            device_id_type=pl.DeviceIdType.MESH,
        )

    def tell():
        return pltpu.make_async_remote_copy(
            src_ref=taken_v.at[0],
            dst_ref=taken_v.at[1],
            send_sem=taken_sem,
            recv_sem=told_sem,
            device_id={"shard": partner},
            device_id_type=pl.DeviceIdType.MESH,
        )

    def reply(off):
        to = lax.rem(me + off, peers)
        return pltpu.make_async_remote_copy(
            src_ref=answer_v.at[to],
            dst_ref=back_v.at[me],
            send_sem=answer_sem.at[off],
            recv_sem=back_sem.at[off],
            device_id={"shard": to},
            device_id_type=pl.DeviceIdType.MESH,
        )

    for c in range(chunks):
        load(c).start()

    barrier = pltpu.get_barrier_semaphore()

    @pl.loop(1, peers)
    def _(off):
        pl.semaphore_signal(
            barrier,
            inc=1,
            device_id={"shard": lax.rem(me + off, peers)},
            device_id_type=pl.DeviceIdType.MESH,
        )

    eye = onehot(iota((tests, tests), 0) == iota((tests, tests), 1))
    cand = dot_nt(eye, cand_ref[...].astype(F32).astype(BF16))
    ids = iota((tests, clusters), 1).astype(F32)
    named = [onehot(cand[:, j : j + 1] == ids) for j in range(per_test)]
    owned = onehot(owner_ref[...] == iota((wide_peers, clusters), 0))
    holder = [dot_nt(chosen, owned) for chosen in named]
    asks = functools.reduce(jnp.add, holder)
    before = onehot(iota((tests, tests), 1) < iota((tests, tests), 0))
    place = dot_nn(before, asks.astype(BF16)) + 1.0
    taken_v[0] = (asks * place).astype(BF16)

    dealt = near * TILE

    def choose(taken):
        spread = onehot(
            (iota((dealt, wide_peers), 0) >> log2(TILE)) + base == iota((dealt, wide_peers), 1)
        )
        tile = onehot(
            (iota((tests, subs * tests), 1) & (tests - 1)) == iota((tests, subs * tests), 0)
        )
        wanted = dot_nn(dot_nt(spread, taken).astype(BF16), tile)
        row = iota((dealt, subs * tests), 0) & (TILE - 1)
        column = iota((dealt, subs * tests), 1)
        same_block = (row >> log2(slots)) == (column >> log2(tests))
        return onehot(same_block & (wanted == ((row & (slots - 1)) + 1).astype(F32)))

    def select_rows(pick, chunk):
        blocks = [chunk[:, q * width : (q + 1) * width] for q in range(subs)]
        block = dot_nn(pick, jnp.concatenate(blocks, axis=0)).astype(BF16)
        return block.reshape(near, TILE, width)

    pick = choose(taken_v[0])
    for c in range(chunks):
        send_v[c] = select_rows(pick, test_ref[:, c * chunk_width : (c + 1) * chunk_width])

    pl.semaphore_wait(barrier, peers - 1)

    tell().start()
    for c in range(chunks):
        cross(c).start()
    for c in range(chunks):

        @pl.loop(1, near)
        def _(off):
            deal(0, c, off).start()

        recv_v[c, me] = send_v[c, member]

    tell().wait_recv()
    pick = choose(taken_v[1])
    square_v[...] = jnp.zeros_like(square_v)
    step = 64

    for c in range(chunks):
        cross(c).wait_recv()
        relay_v[c] = select_rows(pick, far_v[c])

        @pl.loop(1, near)
        def _(off):
            deal(1, c, off).start()

        recv_v[c, partner] = relay_v[c, member]
        load(c).wait()

        @pl.loop(0, capacity // step)
        def _(b):
            at = pl.ds(pl.multiple_of(b * step, step), step)
            total = square_v[at, :]
            for k in range(chunk_width // 128):
                x = train_v[c, at, k * 128 : (k + 1) * 128].astype(F32)
                total += x * x
            square_v[at, :] = total

    mean = jnp.sum(square_v[...].T, axis=0, keepdims=True) / (chunks * chunk_width)
    mine = jnp.where(owner_ref[...] == me, size_ref[...], 0)
    my_size = jnp.sum(mine.astype(F32), axis=1, keepdims=True)
    live = iota((1, capacity), 1).astype(F32) < my_size
    scale = lax.rsqrt(mean + EPS)

    @pl.loop(0, chunks)
    def _(c):
        @pl.loop(1, near)
        def _(off):
            deal(0, c, off).wait_recv()
            deal(1, c, off).wait_recv()

        rows = peers * TILE
        got = recv_v[c].reshape(rows, width)
        which = (iota((rows, width), 0) & (TILE - 1)) >> log2(slots)
        spaced = jnp.concatenate(
            [jnp.where(which == q, got, jnp.zeros_like(got)) for q in range(subs)], axis=1
        )
        part = dot_nt(spaced, train_v[c])

        @pl.when(c == 0)
        def _():
            score_v[...] = part

        @pl.when(c != 0)
        def _():
            score_v[...] += part

    full = score_v[...].reshape(peers, 2, 8, capacity)
    full = (full[:, 0] + full[:, 1]).reshape(peers * 8, capacity)
    turn = slots
    shifted = iota((peers * 8, capacity), 0) & 7
    while turn < 8:
        ahead = pltpu.roll(full, peers * 8 - turn, 0)
        behind = pltpu.roll(full, turn, 0)
        full = full + jnp.where((shifted & turn) == 0, ahead, behind)
        turn *= 2
    full = jnp.where(live, full * scale, 0.0)
    sub = iota((peers * 8, half), 0) & 7
    packed = jnp.where(sub < 4, full[:, :half], full[:, half:])
    answer_v[...] = packed.reshape(peers, 8, half)

    @pl.loop(1, peers)
    def _(off):
        reply(off).start()

    back_v[me] = answer_v[me]

    wide = peers * 8
    spread_back = onehot(
        (iota((wide, wide_peers), 0) >> 3) == iota((wide, wide_peers), 1)
    )
    spot = iota((tests, wide), 1) & 7
    valid = jnp.zeros((tests, 1), F32)
    left, right = [], []
    for j in range(per_test):
        at = dot_nt((holder[j] * place).astype(BF16), spread_back)
        left.append(onehot(at == (spot + 1).astype(F32)))
        right.append(onehot(at == (spot - 3).astype(F32)))
        sizes = jnp.where(named[j] > 0, size_ref[...].astype(F32), 0.0)
        valid += jnp.sum(sizes, axis=1, keepdims=True)
    left = jnp.where(iota((per_test * tests, wide), 1) & 7 < 4, jnp.concatenate(left, axis=0), 0)
    right = jnp.where(
        iota((per_test * tests, wide), 1) & 7 >= 4, jnp.concatenate(right, axis=0), 0
    )
    select = jnp.concatenate([left, right], axis=0).astype(BF16)

    @pl.loop(1, peers)
    def _(off):
        reply(off).wait_recv()

    rest = back_v[...].reshape(wide, half)
    chosen = jnp.zeros((2 * per_test * tests, half), F32)
    for _ in range(3):
        term = rest.astype(BF16)
        chosen += dot_nn(select, term)
        rest = rest - term.astype(F32)

    entries = per_test * tests
    energy = jnp.zeros((tests, 1), F32)
    for j in range(per_test):
        for h in range(2):
            x = chosen[h * entries + j * tests : h * entries + (j + 1) * tests]
            energy += jnp.sum(x * x, axis=1, keepdims=True)
    factor = lax.rsqrt(energy / valid + EPS)
    for j in range(per_test):
        for h in range(2):
            x = chosen[h * entries + j * tests : h * entries + (j + 1) * tests]
            out_ref[:, j, h * half : (h + 1) * half] = x * factor

    @pl.loop(1, peers)
    def _(off):
        reply(off).wait_send()

    @pl.loop(1, near)
    def _(off):
        for c in range(chunks):
            deal(0, c, off).wait_send()
            deal(1, c, off).wait_send()

    for c in range(chunks):
        cross(c).wait_send()
    tell().wait_send()


def shards(test_grads, train_grads, candidates, owner, cluster_sizes):
    peers = lax.axis_size("shard")
    capacity, depth = train_grads.shape
    tests, per_test = candidates.shape
    slots = max(2, -(-tests * per_test // peers))
    subs = TILE // slots
    chunk = depth // CHUNKS
    half = capacity // 2
    near = peers // 2
    vmem = pl.BlockSpec(memory_space=pltpu.VMEM)
    out = pl.pallas_call(
        functools.partial(kernel, peers, slots),
        out_shape=jax.ShapeDtypeStruct((tests, per_test, capacity), F32),
        in_specs=[vmem, pl.BlockSpec(memory_space=pl.ANY), vmem, vmem, vmem],
        out_specs=vmem,
        scratch_shapes=[
            pltpu.VMEM((CHUNKS, capacity, chunk), BF16),
            pltpu.VMEM((CHUNKS, tests, chunk), BF16),
            pltpu.VMEM((2, tests, padded(peers)), BF16),
            pltpu.VMEM((CHUNKS, near, TILE, chunk // subs), BF16),
            pltpu.VMEM((CHUNKS, near, TILE, chunk // subs), BF16),
            pltpu.VMEM((CHUNKS, peers, TILE, chunk // subs), BF16),
            pltpu.VMEM((capacity, 128), F32),
            pltpu.VMEM((peers * TILE, capacity), F32),
            pltpu.VMEM((peers, 8, half), F32),
            pltpu.VMEM((peers, 8, half), F32),
            pltpu.SemaphoreType.DMA((CHUNKS,)),
            pltpu.SemaphoreType.DMA((CHUNKS,)),
            pltpu.SemaphoreType.DMA((CHUNKS,)),
            pltpu.SemaphoreType.DMA,
            pltpu.SemaphoreType.DMA,
            pltpu.SemaphoreType.DMA((2, CHUNKS, near)),
            pltpu.SemaphoreType.DMA((2, CHUNKS, near)),
            pltpu.SemaphoreType.DMA((peers,)),
            pltpu.SemaphoreType.DMA((peers,)),
        ],
        compiler_params=pltpu.CompilerParams(
            collective_id=0, has_side_effects=True, vmem_limit_bytes=56 * 1024 * 1024
        ),
    )(test_grads, train_grads, candidates.T, owner[None, :], cluster_sizes[None, :])
    return out


def solution(mesh):
    in_specs = (
        P(("groups", "shard"), None),
        P(("groups", "shard"), None),
        P(("groups", "shard"), None),
        P("groups"),
        P("groups"),
    )
    out_specs = P(("groups", "shard"), None, None)
    return jax.shard_map(shards, mesh=mesh, in_specs=in_specs, out_specs=out_specs, check_vma=False)
```
